32 devices in a mesh: groups: 2 (over x), band: 16 (over z, y, core).
Axes of the slice: x: 2, y: 2, z: 4, core: 2. Of those that a mesh axis runs over, the one named last changes fastest.
Arguments:
- factor: bfloat16 [32768, 128], P(('groups', 'band')), parts along dimension 0
- near_vals: bfloat16 [512, 5, 64, 64], P(('groups', 'band')), parts along dimension 0, may hold values from 0.049804688 to 4
- far_vals: bfloat16 [32768, 512], P(('groups', 'band')), parts along dimension 0, may hold values from 0.049804688 to 4
- pub_rows: int32 [32, 32], P(('groups', 'band')), parts along dimension 0, may hold values from 0 to 1023
- far_count: int32 [32, 16], P(('groups', 'band')), parts along dimension 0, may hold values from 1 to 32, as said below
Outputs:
- updated: float32 [32768, 128], P(('groups', 'band')), parts along dimension 0
The draws below stay inside these ranges and needn't reach their ends.
There are 2 independent parts, one for each index of `groups`. The reference program is written for one: setup_inputs(seed, part) draws one part's arguments, and reference() takes and returns one part's arrays. A program takes and returns all parts, laid end to end along the dimension named above; each array names one. Nothing has to cross between parts.
Inputs may be any that keep to these rules, and one draw needn't show every extreme that they name: `far_count`: in every row some entry equals 32.
All inputs are finite; a program needn't handle non-finite values.
Results may differ from the reference program's by a relative error of at most 0.0003.
Values may be sent and summed in bfloat16 or wider, within the bound.
A program may use at most 64 MiB of HBM per device.

```python
import math
import jax
import jax.numpy as jnp
from jax import lax

RANK = 128
BLOCK = 64
HALF_BLOCKS = 2
SLOTS = 32
ROWS_DEV = 1024
NROWS = 16384
NBLOCKS = 256
N_BAND = 16


def draw_factor(key, part):
    row_count = ROWS_DEV * N_BAND
    key_base = jax.random.fold_in(key, 11)
    key_cols = jax.random.fold_in(key, 12)
    key_rows = jax.random.fold_in(key, 13)
    values = jax.random.normal(key_base, (row_count, RANK), jnp.float32)
    col_scale = jnp.exp(jax.random.uniform(key_cols, (1, RANK), jnp.float32, 0.0, math.log(10.0))) / math.sqrt(10.0)
    position = jnp.arange(row_count, dtype=jnp.float32)[:, None] / row_count
    row_scale = jnp.exp(math.log(3.0) * position) * jnp.exp(jax.random.uniform(key_rows, (row_count, 1), jnp.float32, -0.35, 0.35))
    read_cols = (2 * HALF_BLOCKS + 1) * BLOCK + N_BAND * SLOTS / 2.0
    base_scale = math.sqrt(read_cols) / row_count / 2.0
    return (values * col_scale * row_scale * base_scale).astype(jnp.bfloat16)


def draw_far_count(key, part):
    counts = jax.random.randint(jax.random.fold_in(key, 21), (N_BAND, N_BAND), 1, SLOTS + 1)
    offset = jax.random.randint(jax.random.fold_in(key, 22), (), 0, N_BAND)
    reader = jnp.arange(N_BAND, dtype=jnp.int32)[:, None]
    owner = jnp.arange(N_BAND, dtype=jnp.int32)[None, :]
    full = owner == (reader + offset) % N_BAND
    return jnp.where(full, SLOTS, counts).astype(jnp.int32)


def plant(array, own_key, low, high):
    place = [jax.random.randint(jax.random.fold_in(own_key, axis), (), 0, length) for axis, length in enumerate(array.shape)]
    main_axis = array.shape.index(max(array.shape))
    next_to = place[:main_axis] + [(place[main_axis] + 1) % array.shape[main_axis]] + place[main_axis + 1:]
    return array.at[tuple(place)].set(low).at[tuple(next_to)].set(high)


def shard_levels(stream_key, extent, pieces, low, top_value):
    factor_of = 1.0
    for dim, blocks in pieces:
        heights = jax.random.uniform(jax.random.fold_in(jax.random.fold_in(stream_key, 6), dim), (blocks,), jnp.float32, low / len(pieces), top_value / len(pieces))
        factor_of = factor_of * jnp.repeat(jnp.exp(heights), extent[dim] // blocks).reshape((-1,) + (1,) * (len(extent) - 1 - dim))
    return factor_of


def setup_inputs(seed: int = 0, part: int = 0) -> dict:
    keys = jax.random.split(jax.random.key(seed), 6)
    part_keys = jax.random.split(jax.random.fold_in(keys[5], part), 6)
    factor = draw_factor(jax.random.fold_in(jax.random.fold_in(keys[5], part), 71), part)
    near_vals = jnp.clip(jnp.exp(math.log(4.0) - 4.3859405 * jax.random.uniform(part_keys[1], (NBLOCKS, 2 * HALF_BLOCKS + 1, BLOCK, BLOCK), jnp.float32) ** shard_levels(part_keys[1], (NBLOCKS, 2 * HALF_BLOCKS + 1, BLOCK, BLOCK), ((0, 16),), -0.2, 0.2)), 0.049804688, 4.0).astype(jnp.bfloat16)
    far_vals = jnp.clip(jnp.exp(math.log(4.0) - 4.3859405 * jax.random.uniform(part_keys[2], (NROWS, N_BAND * SLOTS), jnp.float32) ** shard_levels(part_keys[2], (NROWS, N_BAND * SLOTS), ((0, 16),), -0.2, 0.2)), 0.049804688, 4.0).astype(jnp.bfloat16)
    pub_rows = plant(jax.random.randint(part_keys[3], (N_BAND, SLOTS), 0, ROWS_DEV), jax.random.fold_in(part_keys[3], 1), 0, ROWS_DEV - 1).astype(jnp.int32)
    far_count = draw_far_count(jax.random.fold_in(jax.random.fold_in(keys[5], part), 71), part)
    return {"factor": factor, "near_vals": near_vals, "far_vals": far_vals, "pub_rows": pub_rows, "far_count": far_count}


def reference(factor, near_vals, far_vals, pub_rows, far_count):
    row_count, rank_width = factor.shape
    margin = HALF_BLOCKS * BLOCK
    padded = jnp.pad(factor, ((margin, margin), (0, 0)))
    block_count = row_count // BLOCK
    blocks = padded.reshape(block_count + 2 * HALF_BLOCKS, BLOCK, rank_width)
    near_sum = jnp.zeros((block_count, BLOCK, rank_width), jnp.float32)
    for offset in range(2 * HALF_BLOCKS + 1):
        near_sum = near_sum + jnp.einsum('bij,bjk->bik', near_vals[:, offset].astype(jnp.float32), blocks[offset:offset + block_count].astype(jnp.float32))
    near_sum = near_sum.reshape(row_count, rank_width)
    owners = factor.reshape(N_BAND, ROWS_DEV, rank_width)
    chosen = jax.vmap(lambda owner_rows, picks: jnp.take(owner_rows, picks, axis=0))(owners, pub_rows)
    chosen_flat = chosen.reshape(N_BAND * SLOTS, rank_width)
    slot_index = jnp.arange(N_BAND * SLOTS, dtype=jnp.int32) % SLOTS

    def one_band(inputs):
        band_vals, counts = inputs
        live_slots = slot_index < jnp.repeat(counts, SLOTS)
        masked = jnp.where(live_slots[None, :], band_vals, jnp.zeros((), band_vals.dtype))
        return jnp.dot(masked.astype(jnp.float32), chosen_flat.astype(jnp.float32), preferred_element_type=jnp.float32)
    far_sum = lax.map(one_band, (far_vals.reshape(N_BAND, ROWS_DEV, N_BAND * SLOTS), far_count))
    far_sum = far_sum.reshape(row_count, rank_width)
    gram_matrix = jnp.dot(factor.T.astype(jnp.float32), factor.astype(jnp.float32), preferred_element_type=jnp.float32)
    lower_factor = jnp.linalg.cholesky(gram_matrix)
    inverse = jax.scipy.linalg.cho_solve((lower_factor, True), jnp.eye(rank_width, dtype=jnp.float32))
    return jnp.dot(near_sum + far_sum, inverse, precision=lax.Precision.HIGHEST)
```

```python
import functools

import jax
import jax.numpy as jnp
from jax import lax
from jax.experimental import pallas as pl
from jax.experimental.pallas import tpu as pltpu
from jax.sharding import PartitionSpec as P

BLOCK = 64
HALF_BLOCKS = 2
MESH = pl.DeviceIdType.MESH
TILE = 256


def gather_sums(
    n, far_count, factor, pub, near_hbm, far_hbm, sums, gram_out,
    near, far, shares, parts, total, arrived, picked, before, after,
    local_sem, part_send, part_recv, total_send, total_recv,
    pick_send, pick_recv, edge_send, edge_recv,
):
    group, me = lax.axis_index("groups"), lax.axis_index("band")
    rows, rank = factor.shape
    slots = pub.shape[1]
    height = shares.shape[1]
    margin = HALF_BLOCKS * BLOCK
    block_count = rows // BLOCK

    def peer(step):
        return lax.rem(me + step, n)

    barrier = pltpu.get_barrier_semaphore()

    @pl.loop(1, n)
    def _(step):
        pl.semaphore_signal(
            barrier, inc=1, device_id=(group, peer(step)), device_id_type=MESH
        )

    near_copy = pltpu.make_async_copy(near_hbm, near, local_sem.at[0])
    far_copy = pltpu.make_async_copy(far_hbm, far, local_sem.at[1])
    near_copy.start()
    far_copy.start()

    own = lax.dot_general(
        factor[...], factor[...], (((0,), (0,)), ((), ())),
        preferred_element_type=jnp.float32,
    )
    for index in range(n):
        shares[index] = own[index * height : (index + 1) * height]
    parts[me] = shares[me]

    def part_copy(step):
        return pltpu.make_async_remote_copy(
            src_ref=shares.at[peer(step)], dst_ref=parts.at[me],
            send_sem=part_send.at[step], recv_sem=part_recv.at[step],
            device_id=(group, peer(step)), device_id_type=MESH,
        )

    def total_copy(step):
        return pltpu.make_async_remote_copy(
            src_ref=total.at[me], dst_ref=total.at[me],
            send_sem=total_send.at[step], recv_sem=total_recv.at[step],
            device_id=(group, peer(step)), device_id_type=MESH,
        )

    def pick_copy(step):
        return pltpu.make_async_remote_copy(
            src_ref=arrived.at[me], dst_ref=arrived.at[me],
            send_sem=pick_send.at[step], recv_sem=pick_recv.at[step],
            device_id=(group, peer(step)), device_id_type=MESH,
        )

    pl.semaphore_wait(barrier, n - 1)

    @pl.loop(1, n)
    def _(step):
        part_copy(step).start()

    hit = lax.broadcasted_iota(jnp.int32, (rows, slots), 0) == pub[...]
    chosen = lax.dot_general(
        hit.astype(jnp.float32).astype(jnp.bfloat16), factor[...],
        (((0,), (0,)), ((), ())), preferred_element_type=jnp.float32,
    )
    arrived[me] = chosen.astype(jnp.bfloat16)

    @pl.loop(1, n)
    def _(step):
        pick_copy(step).start()

    down = pltpu.make_async_remote_copy(
        src_ref=factor.at[pl.ds(rows - margin, margin)], dst_ref=before,
        send_sem=edge_send.at[0], recv_sem=edge_recv.at[0],
        device_id=(group, peer(1)), device_id_type=MESH,
    )
    up = pltpu.make_async_remote_copy(
        src_ref=factor.at[pl.ds(0, margin)], dst_ref=after,
        send_sem=edge_send.at[1], recv_sem=edge_recv.at[1],
        device_id=(group, peer(n - 1)), device_id_type=MESH,
    )
    down.start()
    up.start()

    near_copy.wait()

    def near_dot(index, offset, block):
        return jnp.dot(near[index, offset], block, preferred_element_type=jnp.float32)

    @pl.loop(HALF_BLOCKS, block_count - HALF_BLOCKS)
    def _(index):
        value = jnp.zeros((BLOCK, rank), jnp.float32)
        for offset in range(2 * HALF_BLOCKS + 1):
            start = pl.multiple_of((index + offset - HALF_BLOCKS) * BLOCK, BLOCK)
            value = value + near_dot(index, offset, factor[pl.ds(start, BLOCK), :])
        sums[pl.ds(pl.multiple_of(index * BLOCK, BLOCK), BLOCK), :] = value

    @pl.loop(1, n)
    def _(step):
        part_copy(step).wait()

    total[me] = jnp.sum(parts[...], axis=0)

    @pl.loop(1, n)
    def _(step):
        total_copy(step).start()

    down.wait()
    up.wait()
    none = jnp.zeros((margin, rank), jnp.bfloat16)
    first = jnp.where(me > 0, before[...], none)
    last = jnp.where(me < n - 1, after[...], none)

    def block_at(place):
        if place < 0:
            return first[margin + place * BLOCK : margin + (place + 1) * BLOCK]
        if place >= block_count:
            at = (place - block_count) * BLOCK
            return last[at : at + BLOCK]
        return factor[place * BLOCK : (place + 1) * BLOCK, :]

    for index in [*range(HALF_BLOCKS), *range(block_count - HALF_BLOCKS, block_count)]:
        value = jnp.zeros((BLOCK, rank), jnp.float32)
        for offset in range(2 * HALF_BLOCKS + 1):
            value = value + near_dot(index, offset, block_at(index + offset - HALF_BLOCKS))
        sums[index * BLOCK : (index + 1) * BLOCK, :] = value

    @pl.loop(1, n)
    def _(step):
        pick_copy(step).wait()

    slot = lax.broadcasted_iota(jnp.int32, (slots, rank), 0)

    @pl.loop(0, n)
    def _(band):
        live = jnp.where(slot < far_count[0, band], arrived[band].astype(jnp.float32), 0.0)
        at = pl.multiple_of(band * slots, slots)
        picked[pl.ds(at, slots), :] = live.astype(jnp.bfloat16)

    far_copy.wait()

    @pl.loop(0, rows // TILE)
    def _(tile):
        at = pl.ds(pl.multiple_of(tile * TILE, TILE), TILE)
        sums[at, :] += jnp.dot(far[at, :], picked[...], preferred_element_type=jnp.float32)

    @pl.loop(1, n)
    def _(step):
        total_copy(step).wait()

    gram_out[...] = total[...]


def solve(gram, sums, out):
    rank = gram.shape[0]
    slabs = [gram[8 * i : 8 * i + 8, :] for i in range(rank // 8)]
    lane = lax.broadcasted_iota(jnp.int32, (8, rank), 1)
    sub = lax.broadcasted_iota(jnp.int32, (8, rank), 0)
    for k in range(rank):
        home, s = divmod(k, 8)
        at_lane = lane == k
        row = jnp.broadcast_to(slabs[home][s : s + 1, :], (8, rank))
        inv = 1.0 / jnp.broadcast_to(slabs[home][s : s + 1, k : k + 1], (8, rank))
        scaled = jnp.where(at_lane, inv, row * inv)
        new = []
        for i, slab in enumerate(slabs):
            col = jnp.broadcast_to(slab[:, k : k + 1], (8, rank))
            value = jnp.where(at_lane, 0.0, slab) - col * scaled
            if i == home:
                value = jnp.where(sub == s, scaled, value)
            new.append(value)
        slabs = new
    inverse = jnp.concatenate(slabs, axis=0)
    out[...] = jnp.dot(
        sums[...], inverse, precision=lax.Precision.HIGHEST,
        preferred_element_type=jnp.float32,
    )


def shards(factor, near_vals, far_vals, pub_rows, far_count):
    n = lax.axis_size("band")
    rows, rank = factor.shape
    slots = pub_rows.shape[1]
    height = rank // n
    margin = HALF_BLOCKS * BLOCK
    vmem = pl.BlockSpec(memory_space=pltpu.VMEM)
    anywhere = pl.BlockSpec(memory_space=pl.ANY)
    dma = pltpu.SemaphoreType.DMA
    sums, gram = pl.pallas_call(
        functools.partial(gather_sums, n),
        out_shape=(
            jax.ShapeDtypeStruct((rows, rank), jnp.float32),
            jax.ShapeDtypeStruct((n, height, rank), jnp.float32),
        ),
        in_specs=[pl.BlockSpec(memory_space=pltpu.SMEM), vmem, vmem, anywhere, anywhere],
        out_specs=(vmem, vmem),
        scratch_shapes=[
            pltpu.VMEM(near_vals.shape, jnp.bfloat16),
            pltpu.VMEM(far_vals.shape, jnp.bfloat16),
            pltpu.VMEM((n, height, rank), jnp.float32),
            pltpu.VMEM((n, height, rank), jnp.float32),
            pltpu.VMEM((n, height, rank), jnp.float32),
            pltpu.VMEM((n, slots, rank), jnp.bfloat16),
            pltpu.VMEM((n * slots, rank), jnp.bfloat16),
            pltpu.VMEM((margin, rank), jnp.bfloat16),
            pltpu.VMEM((margin, rank), jnp.bfloat16),
            dma((2,)),
            dma((n,)), dma((n,)), dma((n,)), dma((n,)), dma((n,)), dma((n,)),
            dma((2,)), dma((2,)),
        ],
        compiler_params=pltpu.CompilerParams(
            collective_id=0, has_side_effects=True, vmem_limit_bytes=48 << 20
        ),
    )(far_count, factor, pub_rows, near_vals, far_vals)
    return pl.pallas_call(
        solve,
        out_shape=jax.ShapeDtypeStruct((rows, rank), jnp.float32),
        in_specs=[vmem, vmem],
        out_specs=vmem,
        compiler_params=pltpu.CompilerParams(vmem_limit_bytes=32 << 20),
    )(gram.reshape(rank, rank), sums)


def solution(mesh):
    placed = (
        P(("groups", "band"), None),
        P(("groups", "band"), None, None, None),
        P(("groups", "band"), None),
        P(("groups", "band"), None),
        P(("groups", "band"), None),
    )
    return jax.shard_map(
        shards, mesh=mesh, in_specs=placed, out_specs=P(("groups", "band"), None), check_vma=False
    )
```

```python
import functools

import jax
import jax.numpy as jnp
from jax import lax
from jax.experimental import pallas as pl
from jax.experimental.pallas import tpu as pltpu
from jax.sharding import PartitionSpec as P

BLOCK = 64
HALF_BLOCKS = 2
MESH = pl.DeviceIdType.MESH
TILE = 256


def gather_sums(
    n, count_hbm, factor_hbm, pub_hbm, near_hbm, far_hbm, sums, gram_out,
    far_count, factor, pub, near, far, shares, parts, total, arrived, picked, before, after,
    local_sem, part_send, part_recv, total_send, total_recv,
    pick_send, pick_recv, edge_send, edge_recv,
):
    group, me = lax.axis_index("groups"), lax.axis_index("band")
    rows, rank = factor.shape
    slots = pub.shape[1]
    height = shares.shape[1]
    margin = HALF_BLOCKS * BLOCK
    block_count = rows // BLOCK

    def peer(step):
        return lax.rem(me + step, n)

    barrier = pltpu.get_barrier_semaphore()

    @pl.loop(1, n)
    def _(step):
        pl.semaphore_signal(
            barrier, inc=1, device_id=(group, peer(step)), device_id_type=MESH
        )

    near_copy = pltpu.make_async_copy(near_hbm, near, local_sem.at[0])
    far_copy = pltpu.make_async_copy(far_hbm, far, local_sem.at[1])
    factor_copy = pltpu.make_async_copy(factor_hbm, factor, local_sem.at[2])
    pub_copy = pltpu.make_async_copy(pub_hbm, pub, local_sem.at[3])
    count_copy = pltpu.make_async_copy(count_hbm, far_count, local_sem.at[4])
    factor_copy.start()
    pub_copy.start()
    count_copy.start()
    near_copy.start()
    far_copy.start()
    factor_copy.wait()

    own = lax.dot_general(
        factor[...], factor[...], (((0,), (0,)), ((), ())),
        preferred_element_type=jnp.float32,
    )
    for index in range(n):
        shares[index] = own[index * height : (index + 1) * height]
    parts[me] = shares[me]

    def part_copy(step):
        return pltpu.make_async_remote_copy(
            src_ref=shares.at[peer(step)], dst_ref=parts.at[me],
            send_sem=part_send.at[step], recv_sem=part_recv.at[step],
            device_id=(group, peer(step)), device_id_type=MESH,
        )

    def total_copy(step):
        return pltpu.make_async_remote_copy(
            src_ref=total.at[me], dst_ref=total.at[me],
            send_sem=total_send.at[step], recv_sem=total_recv.at[step],
            device_id=(group, peer(step)), device_id_type=MESH,
        )

    def pick_copy(step):
        return pltpu.make_async_remote_copy(
            src_ref=arrived.at[me], dst_ref=arrived.at[me],
            send_sem=pick_send.at[step], recv_sem=pick_recv.at[step],
            device_id=(group, peer(step)), device_id_type=MESH,
        )

    pl.semaphore_wait(barrier, n - 1)

    @pl.loop(1, n)
    def _(step):
        part_copy(step).start()

    pub_copy.wait()
    hit = lax.broadcasted_iota(jnp.int32, (rows, slots), 0) == pub[...]
    chosen = lax.dot_general(
        hit.astype(jnp.float32).astype(jnp.bfloat16), factor[...],
        (((0,), (0,)), ((), ())), preferred_element_type=jnp.float32,
    )
    arrived[me] = chosen.astype(jnp.bfloat16)

    @pl.loop(1, n)
    def _(step):
        pick_copy(step).start()

    down = pltpu.make_async_remote_copy(
        src_ref=factor.at[pl.ds(rows - margin, margin)], dst_ref=before,
        send_sem=edge_send.at[0], recv_sem=edge_recv.at[0],
        device_id=(group, peer(1)), device_id_type=MESH,
    )
    up = pltpu.make_async_remote_copy(
        src_ref=factor.at[pl.ds(0, margin)], dst_ref=after,
        send_sem=edge_send.at[1], recv_sem=edge_recv.at[1],
        device_id=(group, peer(n - 1)), device_id_type=MESH,
    )
    down.start()
    up.start()

    near_copy.wait()

    def near_dot(index, offset, block):
        return jnp.dot(near[index, offset], block, preferred_element_type=jnp.float32)

    @pl.loop(HALF_BLOCKS, block_count - HALF_BLOCKS)
    def _(index):
        value = jnp.zeros((BLOCK, rank), jnp.float32)
        for offset in range(2 * HALF_BLOCKS + 1):
            start = pl.multiple_of((index + offset - HALF_BLOCKS) * BLOCK, BLOCK)
            value = value + near_dot(index, offset, factor[pl.ds(start, BLOCK), :])
        sums[pl.ds(pl.multiple_of(index * BLOCK, BLOCK), BLOCK), :] = value

    @pl.loop(1, n)
    def _(step):
        part_copy(step).wait()

    total[me] = jnp.sum(parts[...], axis=0)

    @pl.loop(1, n)
    def _(step):
        total_copy(step).start()

    down.wait()
    up.wait()
    none = jnp.zeros((margin, rank), jnp.bfloat16)
    first = jnp.where(me > 0, before[...], none)
    last = jnp.where(me < n - 1, after[...], none)

    def block_at(place):
        if place < 0:
            return first[margin + place * BLOCK : margin + (place + 1) * BLOCK]
        if place >= block_count:
            at = (place - block_count) * BLOCK
            return last[at : at + BLOCK]
        return factor[place * BLOCK : (place + 1) * BLOCK, :]

    for index in [*range(HALF_BLOCKS), *range(block_count - HALF_BLOCKS, block_count)]:
        value = jnp.zeros((BLOCK, rank), jnp.float32)
        for offset in range(2 * HALF_BLOCKS + 1):
            value = value + near_dot(index, offset, block_at(index + offset - HALF_BLOCKS))
        sums[index * BLOCK : (index + 1) * BLOCK, :] = value

    @pl.loop(1, n)
    def _(step):
        pick_copy(step).wait()

    count_copy.wait()
    slot = lax.broadcasted_iota(jnp.int32, (slots, rank), 0)

    @pl.loop(0, n)
    def _(band):
        live = jnp.where(slot < far_count[0, band], arrived[band].astype(jnp.float32), 0.0)
        at = pl.multiple_of(band * slots, slots)
        picked[pl.ds(at, slots), :] = live.astype(jnp.bfloat16)

    far_copy.wait()

    @pl.loop(0, rows // TILE)
    def _(tile):
        at = pl.ds(pl.multiple_of(tile * TILE, TILE), TILE)
        sums[at, :] += jnp.dot(far[at, :], picked[...], preferred_element_type=jnp.float32)

    @pl.loop(1, n)
    def _(step):
        total_copy(step).wait()

    gram_out[...] = total[...]


def solve(gram, sums, out, inverse):
    @pl.when(pl.program_id(0) == 0)
    def _():
        inverse[...] = inverted(gram)

    out[...] = jnp.dot(
        sums[...], inverse[...], precision=lax.Precision.HIGHEST,
        preferred_element_type=jnp.float32,
    )


def inverted(gram):
    rank = gram.shape[0]
    slabs = [gram[8 * i : 8 * i + 8, :] for i in range(rank // 8)]
    lane = lax.broadcasted_iota(jnp.int32, (8, rank), 1)
    sub = lax.broadcasted_iota(jnp.int32, (8, rank), 0)
    for home in range(rank // 8):
        base = 8 * home
        panel = slabs[home]
        spread = [
            jnp.broadcast_to(panel[:, base + j : base + j + 1], (8, rank)) for j in range(8)
        ]
        for j in range(8):
            inv = 1.0 / jnp.broadcast_to(spread[j][j : j + 1, :], (8, rank))
            row = jnp.broadcast_to(panel[j : j + 1, :], (8, rank)) * inv
            at_lane, at_row = lane == base + j, sub == j
            scaled = jnp.where(at_lane, inv, row)
            panel = jnp.where(
                at_row, scaled, jnp.where(at_lane, 0.0, panel) - spread[j] * scaled
            )
            for l in range(j + 1, 8):
                ahead = jnp.broadcast_to(spread[l][j : j + 1, :], (8, rank)) * inv
                spread[l] = jnp.where(at_row, ahead, spread[l] - spread[j] * ahead)
        in_block = (lane >= base) & (lane < base + 8)
        rows = [jnp.broadcast_to(panel[j : j + 1, :], (8, rank)) for j in range(8)]
        new = []
        for i, slab in enumerate(slabs):
            value = jnp.where(in_block, 0.0, slab)
            for j in range(8):
                col = jnp.broadcast_to(slab[:, base + j : base + j + 1], (8, rank))
                value = value - col * rows[j]
            new.append(panel if i == home else value)
        slabs = new
    return jnp.concatenate(slabs, axis=0)


def shards(factor, near_vals, far_vals, pub_rows, far_count):
    n = lax.axis_size("band")
    rows, rank = factor.shape
    slots = pub_rows.shape[1]
    height = rank // n
    margin = HALF_BLOCKS * BLOCK
    vmem = pl.BlockSpec(memory_space=pltpu.VMEM)
    anywhere = pl.BlockSpec(memory_space=pltpu.HBM)
    dma = pltpu.SemaphoreType.DMA
    sums, gram = pl.pallas_call(
        functools.partial(gather_sums, n),
        out_shape=(
            jax.ShapeDtypeStruct((rows, rank), jnp.float32),
            jax.ShapeDtypeStruct((n, height, rank), jnp.float32),
        ),
        in_specs=[anywhere] * 5,
        out_specs=(vmem, vmem),
        scratch_shapes=[
            pltpu.SMEM(far_count.shape, jnp.int32),
            pltpu.VMEM(factor.shape, jnp.bfloat16),
            pltpu.VMEM(pub_rows.shape, jnp.int32),
            pltpu.VMEM(near_vals.shape, jnp.bfloat16),
            pltpu.VMEM(far_vals.shape, jnp.bfloat16),
            pltpu.VMEM((n, height, rank), jnp.float32),
            pltpu.VMEM((n, height, rank), jnp.float32),
            pltpu.VMEM((n, height, rank), jnp.float32),
            pltpu.VMEM((n, slots, rank), jnp.bfloat16),
            pltpu.VMEM((n * slots, rank), jnp.bfloat16),
            pltpu.VMEM((margin, rank), jnp.bfloat16),
            pltpu.VMEM((margin, rank), jnp.bfloat16),
            dma((5,)),
            dma((n,)), dma((n,)), dma((n,)), dma((n,)), dma((n,)), dma((n,)),
            dma((2,)), dma((2,)),
        ],
        compiler_params=pltpu.CompilerParams(
            collective_id=0, has_side_effects=True, vmem_limit_bytes=60 << 20
        ),
    )(far_count, factor, pub_rows, near_vals, far_vals)
    return pl.pallas_call(
        solve,
        out_shape=jax.ShapeDtypeStruct((rows, rank), jnp.float32),
        grid=(rows // TILE,),
        in_specs=[
            pl.BlockSpec((rank, rank), lambda i: (0, 0)),
            pl.BlockSpec((TILE, rank), lambda i: (i, 0)),
        ],
        out_specs=pl.BlockSpec((TILE, rank), lambda i: (i, 0)),
        scratch_shapes=[pltpu.VMEM((rank, rank), jnp.float32)],
        compiler_params=pltpu.CompilerParams(vmem_limit_bytes=60 << 20),
    )(gram.reshape(rank, rank), sums)


def solution(mesh):
    placed = (
        P(("groups", "band"), None),
        P(("groups", "band"), None, None, None),
        P(("groups", "band"), None),
        P(("groups", "band"), None),
        P(("groups", "band"), None),
    )
    return jax.shard_map(
        shards, mesh=mesh, in_specs=placed, out_specs=P(("groups", "band"), None), check_vma=False
    )
```

```python
import functools

import jax
import jax.numpy as jnp
from jax import lax
from jax.experimental import pallas as pl
from jax.experimental.pallas import tpu as pltpu
from jax.sharding import PartitionSpec as P

BLOCK = 64
HALF_BLOCKS = 2
MESH = pl.DeviceIdType.MESH
TILE = 512


def gather_sums(
    n, near_n, count_hbm, factor_hbm, pub_hbm, near_hbm, far_hbm, sums_hbm, gram_out,
    sums, far_count, factor, pub, near, far, shares, parts, cross, total, arrived, picked, before, after,
    local_sem, part_send, part_recv, cross_send, cross_recv, total_send, total_recv,
    pick_send, pick_recv, edge_send, edge_recv,
):
    group, me = lax.axis_index("groups"), lax.axis_index("band")
    rows, rank = factor.shape
    slots = pub.shape[1]
    height = shares.shape[1]
    margin = HALF_BLOCKS * BLOCK
    block_count = rows // BLOCK

    far_n = n // near_n
    inner, outer = lax.rem(me, near_n), lax.div(me, near_n)

    def peer(step):
        return lax.rem(me + step, n)

    def beside(step):
        return lax.rem(inner + step, near_n)

    barrier = pltpu.get_barrier_semaphore()

    @pl.loop(1, n)
    def _(step):
        pl.semaphore_signal(
            barrier, inc=1, device_id=(group, peer(step)), device_id_type=MESH
        )

    near_copy = pltpu.make_async_copy(near_hbm, near, local_sem.at[0])
    far_copy = pltpu.make_async_copy(far_hbm, far, local_sem.at[1])
    factor_copy = pltpu.make_async_copy(factor_hbm, factor, local_sem.at[2])
    pub_copy = pltpu.make_async_copy(pub_hbm, pub, local_sem.at[3])
    count_copy = pltpu.make_async_copy(count_hbm, far_count, local_sem.at[4])
    factor_copy.start()
    pub_copy.start()
    count_copy.start()
    near_copy.start()
    far_copy.start()
    factor_copy.wait()

    own = lax.dot_general(
        factor[...], factor[...], (((0,), (0,)), ((), ())),
        preferred_element_type=jnp.float32,
    )
    for index in range(near_n):
        shares[index] = own[index * height : (index + 1) * height]
    parts[inner] = shares[inner]

    def part_copy(step):
        return pltpu.make_async_remote_copy(
            src_ref=shares.at[beside(step)], dst_ref=parts.at[inner],
            send_sem=part_send.at[step], recv_sem=part_recv.at[step],
            device_id=(group, outer * near_n + beside(step)), device_id_type=MESH,
        )

    def cross_copy(step):
        return pltpu.make_async_remote_copy(
            src_ref=cross.at[outer], dst_ref=cross.at[outer],
            send_sem=cross_send.at[step], recv_sem=cross_recv.at[step],
            device_id=(group, peer(step * near_n)), device_id_type=MESH,
        )

    def total_copy(step):
        return pltpu.make_async_remote_copy(
            src_ref=total.at[inner], dst_ref=total.at[inner],
            send_sem=total_send.at[step], recv_sem=total_recv.at[step],
            device_id=(group, outer * near_n + beside(step)), device_id_type=MESH,
        )

    def pick_copy(step):
        return pltpu.make_async_remote_copy(
            src_ref=arrived.at[me], dst_ref=arrived.at[me],
            send_sem=pick_send.at[step], recv_sem=pick_recv.at[step],
            device_id=(group, peer(step)), device_id_type=MESH,
        )

    pl.semaphore_wait(barrier, n - 1)

    for step in range(1, near_n):
        part_copy(step).start()

    pub_copy.wait()
    hit = lax.broadcasted_iota(jnp.int32, (rows, slots), 0) == pub[...]
    chosen = lax.dot_general(
        hit.astype(jnp.float32).astype(jnp.bfloat16), factor[...],
        (((0,), (0,)), ((), ())), preferred_element_type=jnp.float32,
    )
    arrived[me] = chosen.astype(jnp.bfloat16)

    @pl.loop(1, n)
    def _(step):
        pick_copy(step).start()

    down = pltpu.make_async_remote_copy(
        src_ref=factor.at[pl.ds(rows - margin, margin)], dst_ref=before,
        send_sem=edge_send.at[0], recv_sem=edge_recv.at[0],
        device_id=(group, peer(1)), device_id_type=MESH,
    )
    up = pltpu.make_async_remote_copy(
        src_ref=factor.at[pl.ds(0, margin)], dst_ref=after,
        send_sem=edge_send.at[1], recv_sem=edge_recv.at[1],
        device_id=(group, peer(n - 1)), device_id_type=MESH,
    )
    down.start()
    up.start()

    for step in range(1, near_n):
        part_copy(step).wait()

    cross[outer] = jnp.sum(parts[...], axis=0)
    for step in range(1, far_n):
        cross_copy(step).start()

    near_copy.wait()

    def near_dot(index, offset, block):
        return jnp.dot(near[index, offset], block, preferred_element_type=jnp.float32)

    @pl.loop(HALF_BLOCKS, block_count - HALF_BLOCKS)
    def _(index):
        value = jnp.zeros((BLOCK, rank), jnp.float32)
        for offset in range(2 * HALF_BLOCKS + 1):
            start = pl.multiple_of((index + offset - HALF_BLOCKS) * BLOCK, BLOCK)
            value = value + near_dot(index, offset, factor[pl.ds(start, BLOCK), :])
        sums[pl.ds(pl.multiple_of(index * BLOCK, BLOCK), BLOCK), :] = value

    for step in range(1, far_n):
        cross_copy(step).wait()

    total[inner] = jnp.sum(cross[...], axis=0)

    for step in range(1, near_n):
        total_copy(step).start()

    down.wait()
    up.wait()
    none = jnp.zeros((margin, rank), jnp.bfloat16)
    first = jnp.where(me > 0, before[...], none)
    last = jnp.where(me < n - 1, after[...], none)

    def block_at(place):
        if place < 0:
            return first[margin + place * BLOCK : margin + (place + 1) * BLOCK]
        if place >= block_count:
            at = (place - block_count) * BLOCK
            return last[at : at + BLOCK]
        return factor[place * BLOCK : (place + 1) * BLOCK, :]

    for index in [*range(HALF_BLOCKS), *range(block_count - HALF_BLOCKS, block_count)]:
        value = jnp.zeros((BLOCK, rank), jnp.float32)
        for offset in range(2 * HALF_BLOCKS + 1):
            value = value + near_dot(index, offset, block_at(index + offset - HALF_BLOCKS))
        sums[index * BLOCK : (index + 1) * BLOCK, :] = value

    @pl.loop(1, n)
    def _(step):
        pick_copy(step).wait()

    count_copy.wait()
    slot = lax.broadcasted_iota(jnp.int32, (slots, rank), 0)

    @pl.loop(0, n)
    def _(band):
        live = jnp.where(slot < far_count[0, band], arrived[band].astype(jnp.float32), 0.0)
        at = pl.multiple_of(band * slots, slots)
        picked[pl.ds(at, slots), :] = live.astype(jnp.bfloat16)

    far_copy.wait()

    @pl.loop(0, rows // TILE)
    def _(tile):
        at = pl.ds(pl.multiple_of(tile * TILE, TILE), TILE)
        sums[at, :] += jnp.dot(far[at, :], picked[...], preferred_element_type=jnp.float32)

    sums_copy = pltpu.make_async_copy(sums, sums_hbm, local_sem.at[5])
    sums_copy.start()

    for step in range(1, near_n):
        total_copy(step).wait()

    sums_copy.wait()
    gram_out[...] = total[...]


def solve(gram, sums, out, inverse):
    @pl.when(pl.program_id(0) == 0)
    def _():
        inverse[...] = inverted(gram)

    out[...] = jnp.dot(
        sums[...], inverse[...], precision=lax.Precision.HIGHEST,
        preferred_element_type=jnp.float32,
    )


def inverted(gram):
    rank = gram.shape[0]
    slabs = [gram[8 * i : 8 * i + 8, :] for i in range(rank // 8)]
    lane = lax.broadcasted_iota(jnp.int32, (8, rank), 1)
    sub = lax.broadcasted_iota(jnp.int32, (8, rank), 0)
    for home in range(rank // 8):
        base = 8 * home
        panel = slabs[home]
        spread = [
            jnp.broadcast_to(panel[:, base + j : base + j + 1], (8, rank)) for j in range(8)
        ]
        for j in range(8):
            inv = 1.0 / jnp.broadcast_to(spread[j][j : j + 1, :], (8, rank))
            row = jnp.broadcast_to(panel[j : j + 1, :], (8, rank)) * inv
            at_lane, at_row = lane == base + j, sub == j
            scaled = jnp.where(at_lane, inv, row)
            panel = jnp.where(
                at_row, scaled, jnp.where(at_lane, 0.0, panel) - spread[j] * scaled
            )
            for l in range(j + 1, 8):
                ahead = jnp.broadcast_to(spread[l][j : j + 1, :], (8, rank)) * inv
                spread[l] = jnp.where(at_row, ahead, spread[l] - spread[j] * ahead)
        in_block = (lane >= base) & (lane < base + 8)
        rows = [jnp.broadcast_to(panel[j : j + 1, :], (8, rank)) for j in range(8)]
        new = []
        for i, slab in enumerate(slabs):
            value = jnp.where(in_block, 0.0, slab)
            for j in range(8):
                col = jnp.broadcast_to(slab[:, base + j : base + j + 1], (8, rank))
                value = value - col * rows[j]
            new.append(panel if i == home else value)
        slabs = new
    return jnp.concatenate(slabs, axis=0)


def shards(factor, near_vals, far_vals, pub_rows, far_count):
    n = lax.axis_size("band")
    rows, rank = factor.shape
    slots = pub_rows.shape[1]
    near_n = 1
    while 4 * near_n * near_n <= n:
        near_n *= 2
    height = rank // near_n
    margin = HALF_BLOCKS * BLOCK
    vmem = pl.BlockSpec(memory_space=pltpu.VMEM)
    anywhere = pl.BlockSpec(memory_space=pltpu.HBM)
    dma = pltpu.SemaphoreType.DMA
    sums, gram = pl.pallas_call(
        functools.partial(gather_sums, n, near_n),
        out_shape=(
            jax.ShapeDtypeStruct((rows, rank), jnp.float32),
            jax.ShapeDtypeStruct((near_n, height, rank), jnp.float32),
        ),
        in_specs=[anywhere] * 5,
        out_specs=(anywhere, vmem),
        scratch_shapes=[
            pltpu.VMEM((rows, rank), jnp.float32),
            pltpu.SMEM(far_count.shape, jnp.int32),
            pltpu.VMEM(factor.shape, jnp.bfloat16),
            pltpu.VMEM(pub_rows.shape, jnp.int32),
            pltpu.VMEM(near_vals.shape, jnp.bfloat16),
            pltpu.VMEM(far_vals.shape, jnp.bfloat16),
            pltpu.VMEM((near_n, height, rank), jnp.float32),
            pltpu.VMEM((near_n, height, rank), jnp.float32),
            pltpu.VMEM((n // near_n, height, rank), jnp.float32),
            pltpu.VMEM((near_n, height, rank), jnp.float32),
            pltpu.VMEM((n, slots, rank), jnp.bfloat16),
            pltpu.VMEM((n * slots, rank), jnp.bfloat16),
            pltpu.VMEM((margin, rank), jnp.bfloat16),
            pltpu.VMEM((margin, rank), jnp.bfloat16),
            dma((6,)),
            dma((near_n,)), dma((near_n,)), dma((n // near_n,)), dma((n // near_n,)),
            dma((near_n,)), dma((near_n,)), dma((n,)), dma((n,)),
            dma((2,)), dma((2,)),
        ],
        compiler_params=pltpu.CompilerParams(
            collective_id=0, has_side_effects=True, vmem_limit_bytes=60 << 20
        ),
    )(far_count, factor, pub_rows, near_vals, far_vals)
    return pl.pallas_call(
        solve,
        out_shape=jax.ShapeDtypeStruct((rows, rank), jnp.float32),
        grid=(rows // TILE,),
        in_specs=[
            pl.BlockSpec((rank, rank), lambda i: (0, 0)),
            pl.BlockSpec((TILE, rank), lambda i: (i, 0)),
        ],
        out_specs=pl.BlockSpec((TILE, rank), lambda i: (i, 0)),
        scratch_shapes=[pltpu.VMEM((rank, rank), jnp.float32)],
        compiler_params=pltpu.CompilerParams(vmem_limit_bytes=60 << 20),
    )(gram.reshape(rank, rank), sums)


def solution(mesh):
    placed = (
        P(("groups", "band"), None),
        P(("groups", "band"), None, None, None),
        P(("groups", "band"), None),
        P(("groups", "band"), None),
        P(("groups", "band"), None),
    )
    return jax.shard_map(
        shards, mesh=mesh, in_specs=placed, out_specs=P(("groups", "band"), None), check_vma=False
    )
```

```python
import functools

import jax
import jax.numpy as jnp
from jax import lax
from jax.experimental import pallas as pl
from jax.experimental.pallas import tpu as pltpu
from jax.sharding import PartitionSpec as P

BLOCK = 64
HALF_BLOCKS = 2
MESH = pl.DeviceIdType.MESH
TILE = 512


def gather_sums(
    n, near_n, count_hbm, factor_hbm, pub_hbm, near_hbm, far_hbm, sums_hbm, gram_out,
    sums, far_count, factor, pub, near, far, shares, parts, cross, total, arrived, picked, before, after,
    local_sem, part_send, part_recv, cross_send, cross_recv, total_send, total_recv,
    pick_send, pick_recv, band_send, band_recv, edge_send, edge_recv,
):
    group, me = lax.axis_index("groups"), lax.axis_index("band")
    rows, rank = factor.shape
    slots = pub.shape[1]
    height = shares.shape[1]
    margin = HALF_BLOCKS * BLOCK
    block_count = rows // BLOCK

    far_n = n // near_n
    inner, outer = lax.rem(me, near_n), lax.div(me, near_n)

    def peer(step):
        return lax.rem(me + step, n)

    def beside(step):
        return lax.rem(inner + step, near_n)

    barrier = pltpu.get_barrier_semaphore()

    partners = [outer * near_n + beside(step) for step in range(1, near_n)]
    partners += [peer(step * near_n) for step in range(1, far_n)]
    partners += [peer(1), peer(n - 1)]
    for partner in partners:
        pl.semaphore_signal(
            barrier, inc=1, device_id=(group, partner), device_id_type=MESH
        )

    near_copy = pltpu.make_async_copy(near_hbm, near, local_sem.at[0])
    far_copy = pltpu.make_async_copy(far_hbm, far, local_sem.at[1])
    factor_copy = pltpu.make_async_copy(factor_hbm, factor, local_sem.at[2])
    pub_copy = pltpu.make_async_copy(pub_hbm, pub, local_sem.at[3])
    count_copy = pltpu.make_async_copy(count_hbm, far_count, local_sem.at[4])
    factor_copy.start()
    pub_copy.start()
    count_copy.start()
    near_copy.start()
    far_copy.start()
    factor_copy.wait()

    own = lax.dot_general(
        factor[...], factor[...], (((0,), (0,)), ((), ())),
        preferred_element_type=jnp.float32,
    )
    for index in range(near_n):
        shares[index] = own[index * height : (index + 1) * height]
    parts[inner] = shares[inner]

    def part_copy(step):
        return pltpu.make_async_remote_copy(
            src_ref=shares.at[beside(step)], dst_ref=parts.at[inner],
            send_sem=part_send.at[step], recv_sem=part_recv.at[step],
            device_id=(group, outer * near_n + beside(step)), device_id_type=MESH,
        )

    def cross_copy(step):
        return pltpu.make_async_remote_copy(
            src_ref=cross.at[outer], dst_ref=cross.at[outer],
            send_sem=cross_send.at[step], recv_sem=cross_recv.at[step],
            device_id=(group, peer(step * near_n)), device_id_type=MESH,
        )

    def total_copy(step):
        return pltpu.make_async_remote_copy(
            src_ref=total.at[inner], dst_ref=total.at[inner],
            send_sem=total_send.at[step], recv_sem=total_recv.at[step],
            device_id=(group, outer * near_n + beside(step)), device_id_type=MESH,
        )

    def pick_copy(step):
        own_rows = arrived.at[inner, outer]
        return pltpu.make_async_remote_copy(
            src_ref=own_rows, dst_ref=own_rows,
            send_sem=pick_send.at[step], recv_sem=pick_recv.at[step],
            device_id=(group, peer(step * near_n)), device_id_type=MESH,
        )

    def band_copy(step):
        held = arrived.at[inner]
        return pltpu.make_async_remote_copy(
            src_ref=held, dst_ref=held,
            send_sem=band_send.at[step], recv_sem=band_recv.at[step],
            device_id=(group, outer * near_n + beside(step)), device_id_type=MESH,
        )

    pl.semaphore_wait(barrier, len(partners))

    for step in range(1, near_n):
        part_copy(step).start()

    pub_copy.wait()
    hit = lax.broadcasted_iota(jnp.int32, (rows, slots), 0) == pub[...]
    chosen = lax.dot_general(
        hit.astype(jnp.float32).astype(jnp.bfloat16), factor[...],
        (((0,), (0,)), ((), ())), preferred_element_type=jnp.float32,
    )
    arrived[inner, outer] = chosen.astype(jnp.bfloat16)

    for step in range(1, far_n):
        pick_copy(step).start()

    down = pltpu.make_async_remote_copy(
        src_ref=factor.at[pl.ds(rows - margin, margin)], dst_ref=before,
        send_sem=edge_send.at[0], recv_sem=edge_recv.at[0],
        device_id=(group, peer(1)), device_id_type=MESH,
    )
    up = pltpu.make_async_remote_copy(
        src_ref=factor.at[pl.ds(0, margin)], dst_ref=after,
        send_sem=edge_send.at[1], recv_sem=edge_recv.at[1],
        device_id=(group, peer(n - 1)), device_id_type=MESH,
    )
    down.start()
    up.start()

    for step in range(1, near_n):
        part_copy(step).wait()

    cross[outer] = jnp.sum(parts[...], axis=0)
    for step in range(1, far_n):
        cross_copy(step).start()

    for step in range(1, far_n):
        pick_copy(step).wait()
    for step in range(1, near_n):
        band_copy(step).start()

    near_copy.wait()

    def near_dot(index, offset, block):
        return jnp.dot(near[index, offset], block, preferred_element_type=jnp.float32)

    @pl.loop(HALF_BLOCKS, block_count - HALF_BLOCKS)
    def _(index):
        value = jnp.zeros((BLOCK, rank), jnp.float32)
        for offset in range(2 * HALF_BLOCKS + 1):
            start = pl.multiple_of((index + offset - HALF_BLOCKS) * BLOCK, BLOCK)
            value = value + near_dot(index, offset, factor[pl.ds(start, BLOCK), :])
        sums[pl.ds(pl.multiple_of(index * BLOCK, BLOCK), BLOCK), :] = value

    for step in range(1, far_n):
        cross_copy(step).wait()

    total[inner] = jnp.sum(cross[...], axis=0)

    for step in range(1, near_n):
        total_copy(step).start()

    down.wait()
    up.wait()
    none = jnp.zeros((margin, rank), jnp.bfloat16)
    first = jnp.where(me > 0, before[...], none)
    last = jnp.where(me < n - 1, after[...], none)

    def block_at(place):
        if place < 0:
            return first[margin + place * BLOCK : margin + (place + 1) * BLOCK]
        if place >= block_count:
            at = (place - block_count) * BLOCK
            return last[at : at + BLOCK]
        return factor[place * BLOCK : (place + 1) * BLOCK, :]

    for index in [*range(HALF_BLOCKS), *range(block_count - HALF_BLOCKS, block_count)]:
        value = jnp.zeros((BLOCK, rank), jnp.float32)
        for offset in range(2 * HALF_BLOCKS + 1):
            value = value + near_dot(index, offset, block_at(index + offset - HALF_BLOCKS))
        sums[index * BLOCK : (index + 1) * BLOCK, :] = value

    for step in range(1, near_n):
        band_copy(step).wait()

    count_copy.wait()
    slot = lax.broadcasted_iota(jnp.int32, (slots, rank), 0)

    @pl.loop(0, n)
    def _(band):
        live = jnp.where(slot < far_count[0, band], arrived[lax.rem(band, near_n), lax.div(band, near_n)].astype(jnp.float32), 0.0)
        at = pl.multiple_of(band * slots, slots)
        picked[pl.ds(at, slots), :] = live.astype(jnp.bfloat16)

    far_copy.wait()

    @pl.loop(0, rows // TILE)
    def _(tile):
        at = pl.ds(pl.multiple_of(tile * TILE, TILE), TILE)
        sums[at, :] += jnp.dot(far[at, :], picked[...], preferred_element_type=jnp.float32)

    sums_copy = pltpu.make_async_copy(sums, sums_hbm, local_sem.at[5])
    sums_copy.start()

    for step in range(1, near_n):
        total_copy(step).wait()

    sums_copy.wait()
    gram_out[...] = total[...]


def solve(gram, sums, out, inverse):
    @pl.when(pl.program_id(0) == 0)
    def _():
        inverse[...] = inverted(gram)

    out[...] = jnp.dot(
        sums[...], inverse[...], precision=lax.Precision.HIGHEST,
        preferred_element_type=jnp.float32,
    )


def inverted(gram):
    rank = gram.shape[0]
    slabs = [gram[8 * i : 8 * i + 8, :] for i in range(rank // 8)]
    lane = lax.broadcasted_iota(jnp.int32, (8, rank), 1)
    sub = lax.broadcasted_iota(jnp.int32, (8, rank), 0)
    for home in range(rank // 8):
        base = 8 * home
        panel = slabs[home]
        spread = [
            jnp.broadcast_to(panel[:, base + j : base + j + 1], (8, rank)) for j in range(8)
        ]
        for j in range(8):
            inv = 1.0 / jnp.broadcast_to(spread[j][j : j + 1, :], (8, rank))
            row = jnp.broadcast_to(panel[j : j + 1, :], (8, rank)) * inv
            at_lane, at_row = lane == base + j, sub == j
            scaled = jnp.where(at_lane, inv, row)
            panel = jnp.where(
                at_row, scaled, jnp.where(at_lane, 0.0, panel) - spread[j] * scaled
            )
            for l in range(j + 1, 8):
                ahead = jnp.broadcast_to(spread[l][j : j + 1, :], (8, rank)) * inv
                spread[l] = jnp.where(at_row, ahead, spread[l] - spread[j] * ahead)
        in_block = (lane >= base) & (lane < base + 8)
        rows = [jnp.broadcast_to(panel[j : j + 1, :], (8, rank)) for j in range(8)]
        new = []
        for i, slab in enumerate(slabs):
            value = jnp.where(in_block, 0.0, slab)
            for j in range(8):
                col = jnp.broadcast_to(slab[:, base + j : base + j + 1], (8, rank))
                value = value - col * rows[j]
            new.append(panel if i == home else value)
        slabs = new
    return jnp.concatenate(slabs, axis=0)


def shards(factor, near_vals, far_vals, pub_rows, far_count):
    n = lax.axis_size("band")
    rows, rank = factor.shape
    slots = pub_rows.shape[1]
    near_n = 1
    while 4 * near_n * near_n <= n:
        near_n *= 2
    height = rank // near_n
    margin = HALF_BLOCKS * BLOCK
    vmem = pl.BlockSpec(memory_space=pltpu.VMEM)
    anywhere = pl.BlockSpec(memory_space=pltpu.HBM)
    dma = pltpu.SemaphoreType.DMA
    sums, gram = pl.pallas_call(
        functools.partial(gather_sums, n, near_n),
        out_shape=(
            jax.ShapeDtypeStruct((rows, rank), jnp.float32),
            jax.ShapeDtypeStruct((near_n, height, rank), jnp.float32),
        ),
        in_specs=[anywhere] * 5,
        out_specs=(anywhere, vmem),
        scratch_shapes=[
            pltpu.VMEM((rows, rank), jnp.float32),
            pltpu.SMEM(far_count.shape, jnp.int32),
            pltpu.VMEM(factor.shape, jnp.bfloat16),
            pltpu.VMEM(pub_rows.shape, jnp.int32),
            pltpu.VMEM(near_vals.shape, jnp.bfloat16),
            pltpu.VMEM(far_vals.shape, jnp.bfloat16),
            pltpu.VMEM((near_n, height, rank), jnp.float32),
            pltpu.VMEM((near_n, height, rank), jnp.float32),
            pltpu.VMEM((n // near_n, height, rank), jnp.float32),
            pltpu.VMEM((near_n, height, rank), jnp.float32),
            pltpu.VMEM((near_n, n // near_n, slots, rank), jnp.bfloat16),
            pltpu.VMEM((n * slots, rank), jnp.bfloat16),
            pltpu.VMEM((margin, rank), jnp.bfloat16),
            pltpu.VMEM((margin, rank), jnp.bfloat16),
            dma((6,)),
            dma((near_n,)), dma((near_n,)), dma((n // near_n,)), dma((n // near_n,)),
            dma((near_n,)), dma((near_n,)), dma((n // near_n,)), dma((n // near_n,)),
            dma((near_n,)), dma((near_n,)),
            dma((2,)), dma((2,)),
        ],
        compiler_params=pltpu.CompilerParams(
            collective_id=0, has_side_effects=True, vmem_limit_bytes=60 << 20
        ),
    )(far_count, factor, pub_rows, near_vals, far_vals)
    return pl.pallas_call(
        solve,
        out_shape=jax.ShapeDtypeStruct((rows, rank), jnp.float32),
        grid=(rows // TILE,),
        in_specs=[
            pl.BlockSpec((rank, rank), lambda i: (0, 0)),
            pl.BlockSpec((TILE, rank), lambda i: (i, 0)),
        ],
        out_specs=pl.BlockSpec((TILE, rank), lambda i: (i, 0)),
        scratch_shapes=[pltpu.VMEM((rank, rank), jnp.float32)],
        compiler_params=pltpu.CompilerParams(vmem_limit_bytes=60 << 20),
    )(gram.reshape(rank, rank), sums)


def solution(mesh):
    placed = (
        P(("groups", "band"), None),
        P(("groups", "band"), None, None, None),
        P(("groups", "band"), None),
        P(("groups", "band"), None),
        P(("groups", "band"), None),
    )
    return jax.shard_map(
        shards, mesh=mesh, in_specs=placed, out_specs=P(("groups", "band"), None), check_vma=False
    )
```

```python
import functools

import jax
import jax.numpy as jnp
from jax import lax
from jax.experimental import pallas as pl
from jax.experimental.pallas import tpu as pltpu
from jax.sharding import PartitionSpec as P

BLOCK = 64
HALF_BLOCKS = 2
MESH = pl.DeviceIdType.MESH
TILE = 512


def gather_sums(
    n, near_n, count_hbm, factor_hbm, pub_hbm, near_hbm, far_hbm, sums_hbm, gram_out,
    sums, far_count, factor, pub, near, far, shares, parts, cross, total, arrived, picked, before, after,
    local_sem, part_send, part_recv, cross_send, cross_recv, total_send, total_recv,
    pick_send, pick_recv, band_send, band_recv, edge_send, edge_recv,
):
    group, me = lax.axis_index("groups"), lax.axis_index("band")
    rows, rank = factor.shape
    slots = pub.shape[1]
    height = shares.shape[1]
    margin = HALF_BLOCKS * BLOCK
    block_count = rows // BLOCK

    far_n = n // near_n
    inner, outer = lax.rem(me, near_n), lax.div(me, near_n)

    def peer(step):
        return lax.rem(me + step, n)

    def beside(step):
        return lax.rem(inner + step, near_n)

    barrier = pltpu.get_barrier_semaphore()

    partners = [outer * near_n + beside(step) for step in range(1, near_n)]
    partners += [peer(step * near_n) for step in range(1, far_n)]
    partners += [peer(1), peer(n - 1)]
    for partner in partners:
        pl.semaphore_signal(
            barrier, inc=1, device_id=(group, partner), device_id_type=MESH
        )

    near_copy = pltpu.make_async_copy(near_hbm, near, local_sem.at[0])
    far_copy = pltpu.make_async_copy(far_hbm, far, local_sem.at[1])
    factor_copy = pltpu.make_async_copy(factor_hbm, factor, local_sem.at[2])
    pub_copy = pltpu.make_async_copy(pub_hbm, pub, local_sem.at[3])
    count_copy = pltpu.make_async_copy(count_hbm, far_count, local_sem.at[4])
    factor_copy.start()
    pub_copy.start()
    count_copy.start()
    factor_copy.wait()

    own = lax.dot_general(
        factor[...], factor[...], (((0,), (0,)), ((), ())),
        preferred_element_type=jnp.float32,
    )
    for index in range(near_n):
        shares[index] = own[index * height : (index + 1) * height]
    parts[inner] = shares[inner]

    def part_copy(step):
        return pltpu.make_async_remote_copy(
            src_ref=shares.at[beside(step)], dst_ref=parts.at[inner],
            send_sem=part_send.at[step], recv_sem=part_recv.at[step],
            device_id=(group, outer * near_n + beside(step)), device_id_type=MESH,
        )

    def cross_copy(step):
        return pltpu.make_async_remote_copy(
            src_ref=cross.at[outer], dst_ref=cross.at[outer],
            send_sem=cross_send.at[step], recv_sem=cross_recv.at[step],
            device_id=(group, peer(step * near_n)), device_id_type=MESH,
        )

    def total_copy(step):
        return pltpu.make_async_remote_copy(
            src_ref=total.at[inner], dst_ref=total.at[inner],
            send_sem=total_send.at[step], recv_sem=total_recv.at[step],
            device_id=(group, outer * near_n + beside(step)), device_id_type=MESH,
        )

    def pick_copy(step):
        own_rows = arrived.at[inner, outer]
        return pltpu.make_async_remote_copy(
            src_ref=own_rows, dst_ref=own_rows,
            send_sem=pick_send.at[step], recv_sem=pick_recv.at[step],
            device_id=(group, peer(step * near_n)), device_id_type=MESH,
        )

    def band_copy(step):
        held = arrived.at[inner]
        return pltpu.make_async_remote_copy(
            src_ref=held, dst_ref=held,
            send_sem=band_send.at[step], recv_sem=band_recv.at[step],
            device_id=(group, outer * near_n + beside(step)), device_id_type=MESH,
        )

    pub_copy.wait()
    hit = lax.broadcasted_iota(jnp.int32, (rows, slots), 0) == pub[...]
    chosen = lax.dot_general(
        hit.astype(jnp.float32).astype(jnp.bfloat16), factor[...],
        (((0,), (0,)), ((), ())), preferred_element_type=jnp.float32,
    )
    arrived[inner, outer] = chosen.astype(jnp.bfloat16)

    pl.semaphore_wait(barrier, len(partners))

    for step in range(1, near_n):
        part_copy(step).start()

    for step in range(1, far_n):
        pick_copy(step).start()

    down = pltpu.make_async_remote_copy(
        src_ref=factor.at[pl.ds(rows - margin, margin)], dst_ref=before,
        send_sem=edge_send.at[0], recv_sem=edge_recv.at[0],
        device_id=(group, peer(1)), device_id_type=MESH,
    )
    up = pltpu.make_async_remote_copy(
        src_ref=factor.at[pl.ds(0, margin)], dst_ref=after,
        send_sem=edge_send.at[1], recv_sem=edge_recv.at[1],
        device_id=(group, peer(n - 1)), device_id_type=MESH,
    )
    near_copy.start()
    far_copy.start()
    down.start()
    up.start()

    for step in range(1, near_n):
        part_copy(step).wait()

    cross[outer] = jnp.sum(parts[...], axis=0)
    for step in range(1, far_n):
        cross_copy(step).start()

    for step in range(1, far_n):
        pick_copy(step).wait()
    for step in range(1, near_n):
        band_copy(step).start()

    near_copy.wait()

    def near_dot(index, offset, block):
        return jnp.dot(near[index, offset], block, preferred_element_type=jnp.float32)

    @pl.loop(HALF_BLOCKS, block_count - HALF_BLOCKS)
    def _(index):
        value = jnp.zeros((BLOCK, rank), jnp.float32)
        for offset in range(2 * HALF_BLOCKS + 1):
            start = pl.multiple_of((index + offset - HALF_BLOCKS) * BLOCK, BLOCK)
            value = value + near_dot(index, offset, factor[pl.ds(start, BLOCK), :])
        sums[pl.ds(pl.multiple_of(index * BLOCK, BLOCK), BLOCK), :] = value

    for step in range(1, far_n):
        cross_copy(step).wait()

    total[inner] = jnp.sum(cross[...], axis=0)

    for step in range(1, near_n):
        total_copy(step).start()

    down.wait()
    up.wait()
    none = jnp.zeros((margin, rank), jnp.bfloat16)
    first = jnp.where(me > 0, before[...], none)
    last = jnp.where(me < n - 1, after[...], none)

    def block_at(place):
        if place < 0:
            return first[margin + place * BLOCK : margin + (place + 1) * BLOCK]
        if place >= block_count:
            at = (place - block_count) * BLOCK
            return last[at : at + BLOCK]
        return factor[place * BLOCK : (place + 1) * BLOCK, :]

    for index in [*range(HALF_BLOCKS), *range(block_count - HALF_BLOCKS, block_count)]:
        value = jnp.zeros((BLOCK, rank), jnp.float32)
        for offset in range(2 * HALF_BLOCKS + 1):
            value = value + near_dot(index, offset, block_at(index + offset - HALF_BLOCKS))
        sums[index * BLOCK : (index + 1) * BLOCK, :] = value

    for step in range(1, near_n):
        band_copy(step).wait()

    count_copy.wait()
    slot = lax.broadcasted_iota(jnp.int32, (slots, rank), 0)

    @pl.loop(0, n)
    def _(band):
        live = jnp.where(slot < far_count[0, band], arrived[lax.rem(band, near_n), lax.div(band, near_n)].astype(jnp.float32), 0.0)
        at = pl.multiple_of(band * slots, slots)
        picked[pl.ds(at, slots), :] = live.astype(jnp.bfloat16)

    far_copy.wait()

    @pl.loop(0, rows // TILE)
    def _(tile):
        at = pl.ds(pl.multiple_of(tile * TILE, TILE), TILE)
        sums[at, :] += jnp.dot(far[at, :], picked[...], preferred_element_type=jnp.float32)

    sums_copy = pltpu.make_async_copy(sums, sums_hbm, local_sem.at[5])
    sums_copy.start()

    for step in range(1, near_n):
        total_copy(step).wait()

    sums_copy.wait()
    gram_out[...] = total[...]


def solve(gram, sums, out, inverse):
    @pl.when(pl.program_id(0) == 0)
    def _():
        inverse[...] = inverted(gram)

    out[...] = jnp.dot(
        sums[...], inverse[...], precision=lax.Precision.HIGHEST,
        preferred_element_type=jnp.float32,
    )


def inverted(gram):
    rank = gram.shape[0]
    slabs = [gram[8 * i : 8 * i + 8, :] for i in range(rank // 8)]
    lane = lax.broadcasted_iota(jnp.int32, (8, rank), 1)
    sub = lax.broadcasted_iota(jnp.int32, (8, rank), 0)
    for home in range(rank // 8):
        base = 8 * home
        panel = slabs[home]
        spread = [
            jnp.broadcast_to(panel[:, base + j : base + j + 1], (8, rank)) for j in range(8)
        ]
        for j in range(8):
            inv = 1.0 / jnp.broadcast_to(spread[j][j : j + 1, :], (8, rank))
            row = jnp.broadcast_to(panel[j : j + 1, :], (8, rank)) * inv
            at_lane, at_row = lane == base + j, sub == j
            scaled = jnp.where(at_lane, inv, row)
            panel = jnp.where(
                at_row, scaled, jnp.where(at_lane, 0.0, panel) - spread[j] * scaled
            )
            for l in range(j + 1, 8):
                ahead = jnp.broadcast_to(spread[l][j : j + 1, :], (8, rank)) * inv
                spread[l] = jnp.where(at_row, ahead, spread[l] - spread[j] * ahead)
        in_block = (lane >= base) & (lane < base + 8)
        rows = [jnp.broadcast_to(panel[j : j + 1, :], (8, rank)) for j in range(8)]
        new = []
        for i, slab in enumerate(slabs):
            value = jnp.where(in_block, 0.0, slab)
            for j in range(8):
                col = jnp.broadcast_to(slab[:, base + j : base + j + 1], (8, rank))
                value = value - col * rows[j]
            new.append(panel if i == home else value)
        slabs = new
    return jnp.concatenate(slabs, axis=0)


def shards(factor, near_vals, far_vals, pub_rows, far_count):
    n = lax.axis_size("band")
    rows, rank = factor.shape
    slots = pub_rows.shape[1]
    near_n = 1
    while 4 * near_n * near_n <= n:
        near_n *= 2
    height = rank // near_n
    margin = HALF_BLOCKS * BLOCK
    vmem = pl.BlockSpec(memory_space=pltpu.VMEM)
    anywhere = pl.BlockSpec(memory_space=pltpu.HBM)
    dma = pltpu.SemaphoreType.DMA
    sums, gram = pl.pallas_call(
        functools.partial(gather_sums, n, near_n),
        out_shape=(
            jax.ShapeDtypeStruct((rows, rank), jnp.float32),
            jax.ShapeDtypeStruct((near_n, height, rank), jnp.float32),
        ),
        in_specs=[anywhere] * 5,
        out_specs=(anywhere, vmem),
        scratch_shapes=[
            pltpu.VMEM((rows, rank), jnp.float32),
            pltpu.SMEM(far_count.shape, jnp.int32),
            pltpu.VMEM(factor.shape, jnp.bfloat16),
            pltpu.VMEM(pub_rows.shape, jnp.int32),
            pltpu.VMEM(near_vals.shape, jnp.bfloat16),
            pltpu.VMEM(far_vals.shape, jnp.bfloat16),
            pltpu.VMEM((near_n, height, rank), jnp.float32),
            pltpu.VMEM((near_n, height, rank), jnp.float32),
            pltpu.VMEM((n // near_n, height, rank), jnp.float32),
            pltpu.VMEM((near_n, height, rank), jnp.float32),
            pltpu.VMEM((near_n, n // near_n, slots, rank), jnp.bfloat16),
            pltpu.VMEM((n * slots, rank), jnp.bfloat16),
            pltpu.VMEM((margin, rank), jnp.bfloat16),
            pltpu.VMEM((margin, rank), jnp.bfloat16),
            dma((6,)),
            dma((near_n,)), dma((near_n,)), dma((n // near_n,)), dma((n // near_n,)),
            dma((near_n,)), dma((near_n,)), dma((n // near_n,)), dma((n // near_n,)),
            dma((near_n,)), dma((near_n,)),
            dma((2,)), dma((2,)),
        ],
        compiler_params=pltpu.CompilerParams(
            collective_id=0, has_side_effects=True, vmem_limit_bytes=60 << 20
        ),
    )(far_count, factor, pub_rows, near_vals, far_vals)
    return pl.pallas_call(
        solve,
        out_shape=jax.ShapeDtypeStruct((rows, rank), jnp.float32),
        grid=(rows // TILE,),
        in_specs=[
            pl.BlockSpec((rank, rank), lambda i: (0, 0)),
            pl.BlockSpec((TILE, rank), lambda i: (i, 0)),
        ],
        out_specs=pl.BlockSpec((TILE, rank), lambda i: (i, 0)),
        scratch_shapes=[pltpu.VMEM((rank, rank), jnp.float32)],
        compiler_params=pltpu.CompilerParams(vmem_limit_bytes=60 << 20),
    )(gram.reshape(rank, rank), sums)


def solution(mesh):
    placed = (
        P(("groups", "band"), None),
        P(("groups", "band"), None, None, None),
        P(("groups", "band"), None),
        P(("groups", "band"), None),
        P(("groups", "band"), None),
    )
    return jax.shard_map(
        shards, mesh=mesh, in_specs=placed, out_specs=P(("groups", "band"), None), check_vma=False
    )
```
